256 devices in a mesh: stn: 32 (over x, z_lo, core), band: 8 (over z_hi, y).
Axes of the slice: x: 4, y: 4, z: 8 (z_hi: 2, z_lo: 4; z = z_hi * 4 + z_lo), core: 2. Of those that a mesh axis runs over, the one named last changes fastest.
Arguments:
- voltages: bfloat16 [8, 2, 512, 36608], P('band', None, 'stn'), may hold values from -6 to 6
- taps: float32 [16, 256], replicated, may hold values from -1.5 to 1.5
- flags: int32 [512], P('stn'), may hold values 0 or 1
- steer: bfloat16 [256, 2, 256, 256], P('band', None, 'stn'), may hold values from -0.25 to 0.25
- beam_dirs: int32 [128], replicated, may hold values from 0 to 255
Outputs:
- visibilities: bfloat16 [8, 256, 2, 512, 512], P('band', 'stn')
- beams: bfloat16 [8, 256, 2, 2, 128, 128], P('band', 'stn')
The draws below stay inside these ranges and needn't reach their ends.
Inputs may be any that keep to these rules, and one draw needn't show every extreme that they name: `beam_dirs`: each beam names a row of steer.
All inputs are finite; a program needn't handle non-finite values. No bound on the sum of `flags` on one device may be relied on, other than what follows from the above.
Results may differ from the reference program's by a relative error of at most 0.0071.
Values may be sent and summed in bfloat16 or wider, within the bound.
A program may use at most 64 MiB of HBM per device.

```python
import math
import jax
import jax.numpy as jnp
from jax import lax

STATIONS = 256
INPUTS = 512
CHAN = 256
TAPS = 16
FRAMES = 128
SAMPLES = 36608
SUB = 8
BEAMS = 128
DIRS = 256


def touch_ends(entries, stream_key, smallest, top_value):
    spot = [jax.random.randint(jax.random.fold_in(stream_key, axis), (), 0, length) for axis, length in enumerate(entries.shape)]
    main_axis = entries.shape.index(max(entries.shape))
    neighbour = spot[:main_axis] + [(spot[main_axis] + 1) % entries.shape[main_axis]] + spot[main_axis + 1:]
    return entries.at[tuple(spot)].set(smallest).at[tuple(neighbour)].set(top_value)


def level_of(rng, dims, shards, low, largest):
    def one(dim, blocks):
        heights = jax.random.uniform(jax.random.fold_in(jax.random.fold_in(rng, 6), dim), (blocks,), jnp.float32, low / len(shards), largest / len(shards))
        return jnp.repeat(jnp.exp(heights), dims[dim] // blocks).reshape((-1,) + (1,) * (len(dims) - dim - 1))

    level = one(*shards[0])
    for cut in shards[1:]:
        level = level * one(*cut)
    return level


def bell_draw(own_key, shape, scale, limit, shards=(), kind=jnp.bfloat16):
    level = level_of(own_key, shape, shards, -0.22, 0.18) if shards else 1.0
    array = jax.random.normal(own_key, shape, jnp.float32) * scale * level
    return jnp.minimum(jnp.maximum(array, -limit), limit).astype(kind)


def setup_inputs(seed: int = 0) -> dict:
    seeds = jax.random.split(jax.random.key(seed), 6)
    voltages = bell_draw(seeds[0], (SUB, 2, INPUTS, SAMPLES), 1.0, 6.0, ((0, 8), (2, 32)))
    taps = bell_draw(seeds[1], (TAPS, CHAN), 0.25, 1.5, (), jnp.float32)
    flags = touch_ends((jax.random.randint(seeds[2], (INPUTS,), 0, 8) < 7).astype(jnp.int32), jax.random.fold_in(seeds[2], 1), 0, 1)
    steer = bell_draw(seeds[3], (DIRS, 2, CHAN, STATIONS), (2 * STATIONS) ** -0.5, 0.25, ((0, 8), (2, 32)))
    beam_dirs = touch_ends(jax.random.randint(seeds[4], (BEAMS,), 0, DIRS), jax.random.fold_in(seeds[4], 1), 0, DIRS - 1).astype(jnp.int32)
    return {"voltages": voltages, "taps": taps, "flags": flags, "steer": steer, "beam_dirs": beam_dirs}


def dft_matrix_of(chan_len):
    indices = jnp.arange(chan_len, dtype=jnp.int32)
    phase_step = indices[:, None] * indices[None, :] % chan_len
    angle = phase_step.astype(jnp.float32) * (2.0 * math.pi / chan_len)
    normaliser = 1.0 / math.sqrt(chan_len)
    cosine_part = jnp.cos(angle) * normaliser
    sine_part = jnp.sin(angle) * normaliser
    upper_rows = jnp.stack([cosine_part, -sine_part], axis=1)
    lower_rows = jnp.stack([sine_part, cosine_part], axis=1)
    return jnp.stack([upper_rows, lower_rows], axis=0).astype(jnp.bfloat16)

def correlate(spectrum, weights, frames_count):
    hi = lax.Precision.HIGHEST
    count_in = spectrum.shape[1]
    stacked = spectrum.reshape(2 * count_in, frames_count)
    products = jnp.dot(stacked, stacked.T, precision=hi)
    real_part = products[:count_in, :count_in] + products[count_in:, count_in:]
    imag_part = products[count_in:, :count_in] - products[:count_in, count_in:]
    visible = (jnp.stack([real_part, imag_part]) / frames_count).astype(jnp.bfloat16)
    weight_real = weights[:, 0, :]
    weight_imag = weights[:, 1, :]
    weight_block = jnp.concatenate([jnp.concatenate([weight_real, -weight_imag], axis=1), jnp.concatenate([weight_imag, weight_real], axis=1)], axis=0)
    by_pol = spectrum.reshape(2, count_in // 2, 2, frames_count)
    formed = []
    for polarisation in range(2):
        pol_rows = by_pol[:, :, polarisation, :].reshape(count_in, frames_count)
        beam_pol = jnp.dot(weight_block, pol_rows, precision=hi)
        formed.append(beam_pol.reshape(2, weights.shape[0], frames_count))
    return (visible, jnp.stack(formed, axis=1).astype(jnp.bfloat16))

def reference(voltages, taps, flags, steer, beam_dirs):
    dft_matrix = dft_matrix_of(CHAN).astype(jnp.float32)
    keep_mask = flags.astype(jnp.float32)
    picked = jnp.take(steer, beam_dirs, axis=0)
    picked = jnp.transpose(picked, (2, 0, 1, 3)).astype(jnp.float32)

    def one_band(samples):
        frames = samples.astype(jnp.float32).reshape(2, INPUTS, FRAMES + TAPS - 1, CHAN)
        filtered = jnp.zeros((2, INPUTS, FRAMES, CHAN), jnp.float32)
        for tap_step in range(TAPS):
            filtered = filtered + taps[tap_step] * frames[:, :, tap_step:tap_step + FRAMES, :]
        filtered = lax.optimization_barrier(filtered.astype(jnp.bfloat16)).astype(jnp.float32)
        spectra = jnp.einsum('sifk,skoc->oicf', filtered, dft_matrix, precision=lax.Precision.HIGHEST)
        spectra = lax.optimization_barrier(spectra.astype(jnp.bfloat16)).astype(jnp.float32)
        spectra = spectra * keep_mask[None, :, None, None]

        def one_channel(channel):
            spectrum = lax.dynamic_index_in_dim(spectra, channel, 2, keepdims=False)
            weights = lax.dynamic_index_in_dim(picked, channel, 0, keepdims=False)
            return correlate(spectrum, weights, FRAMES)
        return lax.map(one_channel, jnp.arange(CHAN, dtype=jnp.int32))
    visibilities, beams = lax.map(one_band, voltages)
    return (visibilities, beams)
```

```python
import functools
import math

import jax
import jax.numpy as jnp
import numpy as np
from jax import lax
from jax.experimental import pallas as pl
from jax.experimental.pallas import tpu as pltpu
from jax.sharding import PartitionSpec as P

MESH = pl.DeviceIdType.MESH
BF16 = jnp.bfloat16
F32 = jnp.float32

STN = 32
BANDS = 8
INPUTS_HERE = 16
CHAN_HERE = 8
CHAN = 256
TAPS = 16
FRAMES = 128
SAMPLES = 36608
DIRS = 256
BEAMS = 128
STATIONS = 256
INPUTS = 512
HALF_FRAMES = 64
FIRST_COLS = (HALF_FRAMES + TAPS - 1) * CHAN
BLOCK_FRAMES = 8


def dft_rows():
    k = np.arange(CHAN)
    phase = (k[:, None] * k[None, :]) % CHAN
    angle = phase.astype(np.float32) * np.float32(2.0 * math.pi / CHAN)
    scale = np.float32(1.0 / math.sqrt(CHAN))
    c, s = np.cos(angle) * scale, np.sin(angle) * scale
    full = np.stack([np.stack([c, s], 0), np.stack([-s, c], 0)], 0)
    full = full.reshape(2, 2, CHAN, STN, CHAN_HERE).transpose(3, 0, 4, 1, 2)
    return full.reshape(2 * CHAN, 2 * CHAN).astype(jnp.bfloat16)


def pair_rows():
    return (np.arange(INPUTS)[None, :] // 2 == np.arange(STATIONS)[:, None]).astype(jnp.bfloat16)


def peer(m):
    stn = lax.axis_index("stn")
    core, z, x = stn % 2, (stn // 2) % 4, stn // 8
    far, r = (m + 1) % 2, m // 2
    dc, dz, dx = r % 2, (r // 2) % 2, r // 4
    z2 = ((z // 2 + far) % 2) * 2 + (z % 2 + dz) % 2
    to = (((x + dx) % 4) * 4 + z2) * 2 + (core + dc) % 2
    return to, (dx + far + dz + dc) == 0


def turn_kernel(
    volt_hbm, taps_ref, flags_ref, steer_hbm, dirs_ref, dft_hbm, pair_hbm,
    spec_hbm, weight_hbm,
    volt, filt, stage, parcels, table, weights, dft, pairs, keep,
    load_sem, send_sem, recv_sem, steer_send, steer_recv, local_sem,
):
    me, band = lax.axis_index("stn"), lax.axis_index("band")
    row, partner = band % 4, (band + 4) % BANDS
    column_peers = [(band // 4) * 4 + (row + d) % 4 for d in (1, 2, 3)]

    loads = []
    for s in range(2):
        for part, (start, size) in enumerate(((0, FIRST_COLS), (FIRST_COLS, SAMPLES - FIRST_COLS))):
            loads.append(pltpu.make_async_copy(
                volt_hbm.at[0, s, :, pl.ds(start, size)],
                volt.at[s, :, pl.ds(start, size)],
                load_sem.at[2 * s + part]))
    for copy in loads:
        copy.start()
    load_dft = pltpu.make_async_copy(dft_hbm, dft, load_sem.at[4])
    load_dft.start()
    load_pairs = pltpu.make_async_copy(pair_hbm, pairs, load_sem.at[5])
    load_pairs.start()

    def block(b):
        return table.at[pl.ds(pl.multiple_of(b * 512, 512), 512)]

    own_block = pltpu.make_async_copy(steer_hbm, block(band), local_sem.at[0])
    own_block.start()

    barrier = pltpu.get_barrier_semaphore()

    def greet(m, carry):
        to, here = peer(m)

        @pl.when(jnp.logical_not(here))
        def _():
            pl.semaphore_signal(barrier, inc=1, device_id=(to, band), device_id_type=MESH)

        return carry

    lax.fori_loop(0, STN, greet, 0)
    for b in column_peers + [partner]:
        pl.semaphore_signal(barrier, inc=1, device_id=(me, b), device_id_type=MESH)

    def filter_frames(s, first):
        def step(n, carry):
            f0 = first + n * BLOCK_FRAMES
            for h in range(2):
                coef = [taps_ref[t : t + 1, h * 128 : (h + 1) * 128] for t in range(TAPS)]
                acc = [None] * BLOCK_FRAMES
                for g in range(BLOCK_FRAMES + TAPS - 1):
                    at = pl.multiple_of((f0 + g) * CHAN + h * 128, 128)
                    x = volt[s, :, pl.ds(at, 128)].astype(F32)
                    for f in range(max(0, g - TAPS + 1), min(BLOCK_FRAMES - 1, g) + 1):
                        term = coef[g - f] * x
                        acc[f] = term if acc[f] is None else acc[f] + term
                for f in range(BLOCK_FRAMES):
                    to = pl.multiple_of((f0 + f) * INPUTS_HERE, INPUTS_HERE)
                    filt[s, h, pl.ds(to, INPUTS_HERE), :] = acc[f]
            return carry

        lax.fori_loop(0, HALF_FRAMES // BLOCK_FRAMES, step, 0)

    loads[0].wait()
    filter_frames(0, 0)

    pl.semaphore_wait(barrier, STN - 1 + 4)
    steer_sends = []
    for n, b in enumerate([partner] + column_peers):
        steer_sends.append(pltpu.make_async_remote_copy(
            src_ref=steer_hbm, dst_ref=block(band),
            send_sem=steer_send.at[n], recv_sem=steer_recv.at[n],
            device_id=(me, b), device_id_type=MESH))
    for copy in steer_sends:
        copy.start()

    loads[1].wait()
    filter_frames(0, HALF_FRAMES)
    loads[2].wait()
    filter_frames(1, 0)
    loads[3].wait()
    filter_frames(1, HALF_FRAMES)

    lines = lax.broadcasted_iota(jnp.int32, (INPUTS_HERE, 128), 0)
    mask = jnp.zeros((INPUTS_HERE, 128), jnp.int32)
    for i in range(INPUTS_HERE):
        mask = jnp.where(lines == i, flags_ref[i], mask)
    keep[...] = mask.astype(F32)

    load_dft.wait()

    def transform(n, carry):
        rows = []
        for i in range(2):
            parts = [filt[s, h, pl.ds(2 * n + i, FRAMES, stride=INPUTS_HERE), :]
                     for s in range(2) for h in range(2)]
            rows.append(jnp.concatenate(parts, axis=1).astype(BF16))
        out = lax.dot_general(dft[...], jnp.concatenate(rows, axis=0), (((1,), (1,)), ((), ())),
                              preferred_element_type=F32)
        for i in range(2):
            stage[pl.ds(2 * n + i, 2 * CHAN, stride=INPUTS_HERE), :] = out[:, i * 128 : (i + 1) * 128]
        return carry

    lax.fori_loop(0, INPUTS_HERE // 2, transform, 0)

    here_rows = pl.ds(pl.multiple_of(me * INPUTS_HERE, INPUTS_HERE), INPUTS_HERE)

    def parcel(m, to):
        return pltpu.make_async_remote_copy(
            src_ref=parcels.at[m], dst_ref=spec_hbm.at[:, here_rows, :],
            send_sem=send_sem.at[m], recv_sem=recv_sem.at[m],
            device_id=(to, band), device_id_type=MESH)

    def own_parcel(m):
        return pltpu.make_async_copy(parcels.at[m], spec_hbm.at[:, here_rows, :], local_sem.at[1])

    def send(m, carry):
        to, here = peer(m)
        kept = keep[...]
        for j in range(CHAN_HERE):
            for o in range(2):
                at = pl.multiple_of(to * 256 + (o * CHAN_HERE + j) * INPUTS_HERE, INPUTS_HERE)
                tile = stage[pl.ds(at, INPUTS_HERE), :] * kept
                parcels[m, j, :, o * 128 : (o + 1) * 128] = tile.astype(BF16)

        @pl.when(here)
        def _():
            own_parcel(m).start()

        @pl.when(jnp.logical_not(here))
        def _():
            parcel(m, to).start()

        return carry

    lax.fori_loop(0, STN, send, 0)

    steer_sends[0].wait_recv()
    forwards = []
    for n, b in enumerate(column_peers):
        forwards.append(pltpu.make_async_remote_copy(
            src_ref=block(partner), dst_ref=block(partner),
            send_sem=steer_send.at[4 + n], recv_sem=steer_recv.at[4 + n],
            device_id=(me, b), device_id_type=MESH))
    for copy in forwards:
        copy.start()
    own_block.wait()
    for copy in steer_sends[1:] + forwards:
        copy.wait_recv()

    def widen(n, carry):
        at = pl.multiple_of(n * 256, 256)
        rows = table[pl.ds(at, 256), :].astype(F32)
        stage[pl.ds(at, 256), :] = rows[:, :128]
        stage[pl.ds(pl.multiple_of(4096 + n * 256, 256), 256), :] = rows[:, 128:]
        return carry

    lax.fori_loop(0, 16, widen, 0)
    chosen = lax.broadcasted_iota(jnp.int32, (DIRS, BEAMS), 0) == dirs_ref[...]
    chosen = jnp.transpose(chosen.astype(F32)).astype(BF16)
    load_pairs.wait()

    def pick(n, carry):
        for o in range(2):
            halves = [stage[pl.ds(h * 4096 + o * CHAN_HERE + n, DIRS, stride=16), :] for h in range(2)]
            rows = jnp.concatenate(halves, axis=1).astype(BF16)
            picked = jnp.dot(chosen, rows, preferred_element_type=F32).astype(BF16)
            spread = jnp.dot(picked, pairs[...], preferred_element_type=F32)
            weights[n, o * BEAMS : (o + 1) * BEAMS, :] = spread.astype(BF16)
        return carry

    lax.fori_loop(0, CHAN_HERE, pick, 0)
    out_weights = pltpu.make_async_copy(weights, weight_hbm, local_sem.at[2])
    out_weights.start()

    for copy in steer_sends + forwards:
        copy.wait_send()

    def finish(m, carry):
        to, here = peer(m)

        @pl.when(here)
        def _():
            own_parcel(m).wait()

        @pl.when(jnp.logical_not(here))
        def _():
            parcel(m, to).wait()

        return carry

    lax.fori_loop(0, STN, finish, 0)
    out_weights.wait()


def form_kernel(spec_ref, weight_ref, vis_ref, beam_ref):
    rows = spec_ref[0]
    real, imag = rows[:, :FRAMES], rows[:, FRAMES:]
    turned = jnp.concatenate([imag, -real], axis=1)
    nt = (((1,), (1,)), ((), ()))
    scale = 1.0 / FRAMES
    for o, left in enumerate((rows, turned)):
        products = lax.dot_general(left, rows, nt, preferred_element_type=F32)
        vis_ref[0, 0, o] = (products * scale).astype(BF16)
    weight = weight_ref[0]
    lane = lax.broadcasted_iota(jnp.int32, weight.shape, 1)
    for p in range(2):
        mine = jnp.where(lane % 2 == p, weight, jnp.zeros_like(weight))
        formed = jnp.dot(mine, rows, preferred_element_type=F32)
        rr, ri = formed[:BEAMS, :FRAMES], formed[:BEAMS, FRAMES:]
        ir, ii = formed[BEAMS:, :FRAMES], formed[BEAMS:, FRAMES:]
        beam_ref[0, 0, 0, p] = (rr - ii).astype(BF16)
        beam_ref[0, 0, 1, p] = (ri + ir).astype(BF16)


def body(dft, pairs, voltages, taps, flags, steer, beam_dirs):
    hbm = pl.BlockSpec(memory_space=pl.ANY)
    vmem = pl.BlockSpec(memory_space=pltpu.VMEM)
    smem = pl.BlockSpec(memory_space=pltpu.SMEM)
    spectra, weights = pl.pallas_call(
        turn_kernel,
        out_shape=(
            jax.ShapeDtypeStruct((CHAN_HERE, INPUTS, 2 * FRAMES), BF16),
            jax.ShapeDtypeStruct((CHAN_HERE, 2 * BEAMS, INPUTS), BF16),
        ),
        in_specs=[hbm, vmem, smem, hbm, vmem, hbm, hbm],
        out_specs=(hbm, hbm),
        scratch_shapes=[
            pltpu.VMEM((2, INPUTS_HERE, SAMPLES), BF16),
            pltpu.VMEM((2, 2, FRAMES * INPUTS_HERE, 128), F32),
            pltpu.VMEM((2 * CHAN * INPUTS_HERE, 128), F32),
            pltpu.VMEM((STN, CHAN_HERE, INPUTS_HERE, 2 * FRAMES), BF16),
            pltpu.VMEM((DIRS * 16, STATIONS), BF16),
            pltpu.VMEM((CHAN_HERE, 2 * BEAMS, INPUTS), BF16),
            pltpu.VMEM((2 * CHAN, 2 * CHAN), BF16),
            pltpu.VMEM((STATIONS, INPUTS), BF16),
            pltpu.VMEM((INPUTS_HERE, 128), F32),
            pltpu.SemaphoreType.DMA((6,)),
            pltpu.SemaphoreType.DMA((STN,)),
            pltpu.SemaphoreType.DMA((STN,)),
            pltpu.SemaphoreType.DMA((7,)),
            pltpu.SemaphoreType.DMA((7,)),
            pltpu.SemaphoreType.DMA((3,)),
        ],
        compiler_params=pltpu.CompilerParams(
            collective_id=0, has_side_effects=True, vmem_limit_bytes=62 * 2**20
        ),
        cost_estimate=pl.CostEstimate(
            flops=1_200_000_000, bytes_accessed=12_000_000, transcendentals=0
        ),
        name="turn",
    )(voltages, taps, flags, steer.reshape(512, STATIONS), beam_dirs.reshape(1, BEAMS), dft, pairs)
    return pl.pallas_call(
        form_kernel,
        grid=(CHAN_HERE,),
        out_shape=(
            jax.ShapeDtypeStruct((1, CHAN_HERE, 2, INPUTS, INPUTS), BF16),
            jax.ShapeDtypeStruct((1, CHAN_HERE, 2, 2, BEAMS, FRAMES), BF16),
        ),
        in_specs=[
            pl.BlockSpec((1, INPUTS, 2 * FRAMES), lambda c: (c, 0, 0)),
            pl.BlockSpec((1, 2 * BEAMS, INPUTS), lambda c: (c, 0, 0)),
        ],
        out_specs=(
            pl.BlockSpec((1, 1, 2, INPUTS, INPUTS), lambda c: (0, c, 0, 0, 0)),
            pl.BlockSpec((1, 1, 2, 2, BEAMS, FRAMES), lambda c: (0, c, 0, 0, 0, 0)),
        ),
        compiler_params=pltpu.CompilerParams(vmem_limit_bytes=48 * 2**20),
        cost_estimate=pl.CostEstimate(
            flops=3_300_000_000, bytes_accessed=14_000_000, transcendentals=0
        ),
        name="form",
    )(spectra, weights)


def solution(mesh):
    dft, pairs = dft_rows(), pair_rows()

    def whole(*args):
        return jax.shard_map(
            functools.partial(body, jnp.asarray(dft), jnp.asarray(pairs)),
            mesh=mesh,
            in_specs=(P("band", None, "stn", None), P(), P("stn"), P("band", None, "stn", None), P()),
            out_specs=(P("band", "stn", None, None, None), P("band", "stn", None, None, None, None)),
            check_vma=False,
        )(*args)

    return whole
```

```python
import functools
import math

import jax
import jax.numpy as jnp
import numpy as np
from jax import lax
from jax.experimental import pallas as pl
from jax.experimental.pallas import tpu as pltpu
from jax.sharding import PartitionSpec as P

MESH = pl.DeviceIdType.MESH
BF16 = jnp.bfloat16
F32 = jnp.float32

STN = 32
BANDS = 8
INPUTS_HERE = 16
CHAN_HERE = 8
CHAN = 256
TAPS = 16
FRAMES = 128
SAMPLES = 36608
DIRS = 256
BEAMS = 128
STATIONS = 256
INPUTS = 512
HALF_FRAMES = 64
FIRST_COLS = (HALF_FRAMES + TAPS - 1) * CHAN
BLOCK_FRAMES = 8


def dft_rows():
    k = np.arange(CHAN)
    phase = (k[:, None] * k[None, :]) % CHAN
    angle = phase.astype(np.float32) * np.float32(2.0 * math.pi / CHAN)
    scale = np.float32(1.0 / math.sqrt(CHAN))
    c, s = np.cos(angle) * scale, np.sin(angle) * scale
    full = np.stack([np.stack([c, s], 0), np.stack([-s, c], 0)], 0)
    full = full.reshape(2, 2, CHAN, STN, CHAN_HERE).transpose(3, 0, 4, 1, 2)
    return full.reshape(2 * CHAN, 2 * CHAN).astype(jnp.bfloat16)


def peer(m):
    stn = lax.axis_index("stn")
    core, z, x = stn % 2, (stn // 2) % 4, stn // 8
    far, r = (m + 1) % 2, m // 2
    dc, dz, dx = r % 2, (r // 2) % 2, r // 4
    z2 = ((z // 2 + far) % 2) * 2 + (z % 2 + dz) % 2
    to = (((x + dx) % 4) * 4 + z2) * 2 + (core + dc) % 2
    return to, (dx + far + dz + dc) == 0


def turn_kernel(
    volt_hbm, taps_ref, flags_ref, steer_hbm, dirs_ref, dft_hbm,
    spec_hbm, weight_hbm,
    volt, filt, stage, parcels, table, weights, dft, keep,
    load_sem, send_sem, recv_sem, steer_send, steer_recv, local_sem,
):
    me, band = lax.axis_index("stn"), lax.axis_index("band")
    row, partner = band % 4, (band + 4) % BANDS
    column_peers = [(band // 4) * 4 + (row + d) % 4 for d in (1, 2, 3)]

    loads = []
    for s in range(2):
        for part, (start, size) in enumerate(((0, FIRST_COLS), (FIRST_COLS, SAMPLES - FIRST_COLS))):
            loads.append(pltpu.make_async_copy(
                volt_hbm.at[0, s, :, pl.ds(start, size)],
                volt.at[s, :, pl.ds(start, size)],
                load_sem.at[2 * s + part]))
    for copy in loads:
        copy.start()
    load_dft = pltpu.make_async_copy(dft_hbm, dft, load_sem.at[4])
    load_dft.start()

    def block(b):
        return table.at[pl.ds(pl.multiple_of(b * 512, 512), 512)]

    own_block = pltpu.make_async_copy(steer_hbm, block(band), local_sem.at[0])
    own_block.start()

    barrier = pltpu.get_barrier_semaphore()

    def greet(m, carry):
        to, here = peer(m)

        @pl.when(jnp.logical_not(here))
        def _():
            pl.semaphore_signal(barrier, inc=1, device_id=(to, band), device_id_type=MESH)

        return carry

    lax.fori_loop(0, STN, greet, 0)
    for b in column_peers + [partner]:
        pl.semaphore_signal(barrier, inc=1, device_id=(me, b), device_id_type=MESH)

    def filter_frames(s, first):
        def step(n, carry):
            f0 = first + n * BLOCK_FRAMES
            for h in range(2):
                coef = [taps_ref[t : t + 1, h * 128 : (h + 1) * 128] for t in range(TAPS)]
                acc = [None] * BLOCK_FRAMES
                for g in range(BLOCK_FRAMES + TAPS - 1):
                    at = pl.multiple_of((f0 + g) * CHAN + h * 128, 128)
                    x = volt[s, :, pl.ds(at, 128)].astype(F32)
                    for f in range(max(0, g - TAPS + 1), min(BLOCK_FRAMES - 1, g) + 1):
                        term = coef[g - f] * x
                        acc[f] = term if acc[f] is None else acc[f] + term
                for f in range(BLOCK_FRAMES):
                    to = pl.multiple_of((f0 + f) * INPUTS_HERE, INPUTS_HERE)
                    filt[s, h, pl.ds(to, INPUTS_HERE), :] = acc[f]
            return carry

        lax.fori_loop(0, HALF_FRAMES // BLOCK_FRAMES, step, 0)

    loads[0].wait()
    filter_frames(0, 0)

    pl.semaphore_wait(barrier, STN - 1 + 4)
    steer_sends = []
    for n, b in enumerate([partner] + column_peers):
        steer_sends.append(pltpu.make_async_remote_copy(
            src_ref=steer_hbm, dst_ref=block(band),
            send_sem=steer_send.at[n], recv_sem=steer_recv.at[n],
            device_id=(me, b), device_id_type=MESH))
    for copy in steer_sends:
        copy.start()

    loads[1].wait()
    filter_frames(0, HALF_FRAMES)
    loads[2].wait()
    filter_frames(1, 0)
    loads[3].wait()
    filter_frames(1, HALF_FRAMES)

    lines = lax.broadcasted_iota(jnp.int32, (INPUTS_HERE, 128), 0)
    mask = jnp.zeros((INPUTS_HERE, 128), jnp.int32)
    for i in range(INPUTS_HERE):
        mask = jnp.where(lines == i, flags_ref[i], mask)
    keep[...] = mask.astype(F32)

    load_dft.wait()

    def transform(n, carry):
        rows = []
        for i in range(2):
            parts = [filt[s, h, pl.ds(2 * n + i, FRAMES, stride=INPUTS_HERE), :]
                     for s in range(2) for h in range(2)]
            rows.append(jnp.concatenate(parts, axis=1).astype(BF16))
        out = lax.dot_general(dft[...], jnp.concatenate(rows, axis=0), (((1,), (1,)), ((), ())),
                              preferred_element_type=F32)
        for i in range(2):
            stage[pl.ds(2 * n + i, 2 * CHAN, stride=INPUTS_HERE), :] = out[:, i * 128 : (i + 1) * 128]
        return carry

    lax.fori_loop(0, INPUTS_HERE // 2, transform, 0)

    here_rows = pl.ds(pl.multiple_of(me * INPUTS_HERE, INPUTS_HERE), INPUTS_HERE)

    def parcel(m, to):
        return pltpu.make_async_remote_copy(
            src_ref=parcels.at[m], dst_ref=spec_hbm.at[:, here_rows, :],
            send_sem=send_sem.at[m], recv_sem=recv_sem.at[m],
            device_id=(to, band), device_id_type=MESH)

    def own_parcel(m):
        return pltpu.make_async_copy(parcels.at[m], spec_hbm.at[:, here_rows, :], local_sem.at[1])

    def send(m, carry):
        to, here = peer(m)
        kept = keep[...]
        for j in range(CHAN_HERE):
            for o in range(2):
                at = pl.multiple_of(to * 256 + (o * CHAN_HERE + j) * INPUTS_HERE, INPUTS_HERE)
                tile = stage[pl.ds(at, INPUTS_HERE), :] * kept
                parcels[m, j, :, o * 128 : (o + 1) * 128] = tile.astype(BF16)

        @pl.when(here)
        def _():
            own_parcel(m).start()

        @pl.when(jnp.logical_not(here))
        def _():
            parcel(m, to).start()

        return carry

    lax.fori_loop(0, STN, send, 0)

    steer_sends[0].wait_recv()
    forwards = []
    for n, b in enumerate(column_peers):
        forwards.append(pltpu.make_async_remote_copy(
            src_ref=block(partner), dst_ref=block(partner),
            send_sem=steer_send.at[4 + n], recv_sem=steer_recv.at[4 + n],
            device_id=(me, b), device_id_type=MESH))
    for copy in forwards:
        copy.start()
    own_block.wait()
    for copy in steer_sends[1:] + forwards:
        copy.wait_recv()

    def widen(n, carry):
        at = pl.multiple_of(n * 256, 256)
        rows = table[pl.ds(at, 256), :].astype(F32)
        stage[pl.ds(at, 256), :] = rows[:, :128]
        stage[pl.ds(pl.multiple_of(4096 + n * 256, 256), 256), :] = rows[:, 128:]
        return carry

    lax.fori_loop(0, 16, widen, 0)
    chosen = lax.broadcasted_iota(jnp.int32, (DIRS, BEAMS), 0) == dirs_ref[...]
    chosen = jnp.transpose(chosen.astype(F32)).astype(BF16)
    pairs = (lax.broadcasted_iota(jnp.int32, (STATIONS, INPUTS), 1) // 2
             == lax.broadcasted_iota(jnp.int32, (STATIONS, INPUTS), 0)).astype(F32).astype(BF16)

    def pick(n, carry):
        for o in range(2):
            halves = [stage[pl.ds(h * 4096 + o * CHAN_HERE + n, DIRS, stride=16), :] for h in range(2)]
            rows = jnp.concatenate(halves, axis=1).astype(BF16)
            picked = jnp.dot(chosen, rows, preferred_element_type=F32).astype(BF16)
            spread = jnp.dot(picked, pairs, preferred_element_type=F32)
            weights[n, o * BEAMS : (o + 1) * BEAMS, :] = spread.astype(BF16)
        return carry

    lax.fori_loop(0, CHAN_HERE, pick, 0)
    out_weights = pltpu.make_async_copy(weights, weight_hbm, local_sem.at[2])
    out_weights.start()

    for copy in steer_sends + forwards:
        copy.wait_send()

    def finish(m, carry):
        to, here = peer(m)

        @pl.when(here)
        def _():
            own_parcel(m).wait()

        @pl.when(jnp.logical_not(here))
        def _():
            parcel(m, to).wait()

        return carry

    lax.fori_loop(0, STN, finish, 0)
    out_weights.wait()


def form_kernel(spec_ref, weight_ref, vis_hbm, beam_hbm, vis, beam, vis_sem, beam_sem):
    nt = (((1,), (1,)), ((), ()))
    scale = 1.0 / FRAMES
    lane = lax.broadcasted_iota(jnp.int32, (2 * BEAMS, INPUTS), 1)
    writes = []
    for c in range(CHAN_HERE):
        rows = spec_ref[c]
        real, imag = rows[:, :FRAMES], rows[:, FRAMES:]
        for o in range(2):
            left = rows if o == 0 else jnp.concatenate([imag, -real], axis=1)
            products = lax.dot_general(left, rows, nt, preferred_element_type=F32)
            vis[c, o] = (products * scale).astype(BF16)
            writes.append(pltpu.make_async_copy(vis.at[c, o], vis_hbm.at[0, c, o], vis_sem.at[c, o]))
            writes[-1].start()
        weight = weight_ref[c]
        for p in range(2):
            mine = jnp.where(lane % 2 == p, weight, jnp.zeros_like(weight))
            formed = jnp.dot(mine, rows, preferred_element_type=F32)
            rr, ri = formed[:BEAMS, :FRAMES], formed[:BEAMS, FRAMES:]
            ir, ii = formed[BEAMS:, :FRAMES], formed[BEAMS:, FRAMES:]
            beam[c, 0, p] = (rr - ii).astype(BF16)
            beam[c, 1, p] = (ri + ir).astype(BF16)
        writes.append(pltpu.make_async_copy(beam.at[c], beam_hbm.at[0, c], beam_sem.at[c]))
        writes[-1].start()
    for copy in writes:
        copy.wait()


def body(dft, voltages, taps, flags, steer, beam_dirs):
    hbm = pl.BlockSpec(memory_space=pltpu.HBM)
    anywhere = pl.BlockSpec(memory_space=pl.ANY)
    vmem = pl.BlockSpec(memory_space=pltpu.VMEM)
    smem = pl.BlockSpec(memory_space=pltpu.SMEM)
    spectra, weights = pl.pallas_call(
        turn_kernel,
        out_shape=(
            jax.ShapeDtypeStruct((CHAN_HERE, INPUTS, 2 * FRAMES), BF16),
            jax.ShapeDtypeStruct((CHAN_HERE, 2 * BEAMS, INPUTS), BF16),
        ),
        in_specs=[hbm, vmem, smem, hbm, vmem, anywhere],
        out_specs=(anywhere, anywhere),
        scratch_shapes=[
            pltpu.VMEM((2, INPUTS_HERE, SAMPLES), BF16),
            pltpu.VMEM((2, 2, FRAMES * INPUTS_HERE, 128), F32),
            pltpu.VMEM((2 * CHAN * INPUTS_HERE, 128), F32),
            pltpu.VMEM((STN, CHAN_HERE, INPUTS_HERE, 2 * FRAMES), BF16),
            pltpu.VMEM((DIRS * 16, STATIONS), BF16),
            pltpu.VMEM((CHAN_HERE, 2 * BEAMS, INPUTS), BF16),
            pltpu.VMEM((2 * CHAN, 2 * CHAN), BF16),
            pltpu.VMEM((INPUTS_HERE, 128), F32),
            pltpu.SemaphoreType.DMA((5,)),
            pltpu.SemaphoreType.DMA((STN,)),
            pltpu.SemaphoreType.DMA((STN,)),
            pltpu.SemaphoreType.DMA((7,)),
            pltpu.SemaphoreType.DMA((7,)),
            pltpu.SemaphoreType.DMA((3,)),
        ],
        compiler_params=pltpu.CompilerParams(
            collective_id=0, has_side_effects=True, vmem_limit_bytes=36 * 2**20
        ),
        cost_estimate=pl.CostEstimate(
            flops=1_200_000_000, bytes_accessed=12_000_000, transcendentals=0
        ),
        name="turn",
    )(*[pltpu.with_memory_space_constraint(v, pltpu.HBM) for v in (
        voltages, taps, flags, steer.reshape(512, STATIONS), beam_dirs.reshape(1, BEAMS), dft)])
    return pl.pallas_call(
        form_kernel,
        out_shape=(
            jax.ShapeDtypeStruct((1, CHAN_HERE, 2, INPUTS, INPUTS), BF16),
            jax.ShapeDtypeStruct((1, CHAN_HERE, 2, 2, BEAMS, FRAMES), BF16),
        ),
        in_specs=[vmem, vmem],
        out_specs=(anywhere, anywhere),
        scratch_shapes=[
            pltpu.VMEM((CHAN_HERE, 2, INPUTS, INPUTS), BF16),
            pltpu.VMEM((CHAN_HERE, 2, 2, BEAMS, FRAMES), BF16),
            pltpu.SemaphoreType.DMA((CHAN_HERE, 2)),
            pltpu.SemaphoreType.DMA((CHAN_HERE,)),
        ],
        compiler_params=pltpu.CompilerParams(vmem_limit_bytes=32 * 2**20),
        cost_estimate=pl.CostEstimate(
            flops=3_300_000_000, bytes_accessed=14_000_000, transcendentals=0
        ),
        name="form",
    )(spectra, weights)


def solution(mesh):
    dft = dft_rows()

    def whole(*args):
        return jax.shard_map(
            functools.partial(body, jnp.asarray(dft)),
            mesh=mesh,
            in_specs=(P("band", None, "stn", None), P(), P("stn"), P("band", None, "stn", None), P()),
            out_specs=(P("band", "stn", None, None, None), P("band", "stn", None, None, None, None)),
            check_vma=False,
        )(*args)

    return whole
```

```python
import functools
import math

import jax
import jax.numpy as jnp
import numpy as np
from jax import lax
from jax.experimental import pallas as pl
from jax.experimental.pallas import tpu as pltpu
from jax.sharding import PartitionSpec as P

MESH = pl.DeviceIdType.MESH
BF16 = jnp.bfloat16
F32 = jnp.float32

STN = 32
BANDS = 8
INPUTS_HERE = 16
CHAN_HERE = 8
CHAN = 256
TAPS = 16
FRAMES = 128
SAMPLES = 36608
DIRS = 256
BEAMS = 128
STATIONS = 256
INPUTS = 512
HALF_FRAMES = 64
FIRST_COLS = (HALF_FRAMES + TAPS - 1) * CHAN
BLOCK_FRAMES = 16


def dft_rows():
    k = np.arange(CHAN)
    phase = (k[:, None] * k[None, :]) % CHAN
    angle = phase.astype(np.float32) * np.float32(2.0 * math.pi / CHAN)
    scale = np.float32(1.0 / math.sqrt(CHAN))
    c, s = np.cos(angle) * scale, np.sin(angle) * scale
    full = np.stack([np.stack([c, s], 0), np.stack([-s, c], 0)], 0)
    full = full.reshape(2, 2, CHAN, STN, CHAN_HERE).transpose(3, 0, 4, 1, 2)
    return full.reshape(2 * CHAN, 2 * CHAN).astype(jnp.bfloat16)


def peer(m):
    stn = lax.axis_index("stn")
    core, z, x = stn % 2, (stn // 2) % 4, stn // 8
    far, r = (m + 1) % 2, m // 2
    dc, dz, dx = r % 2, (r // 2) % 2, r // 4
    z2 = ((z // 2 + far) % 2) * 2 + (z % 2 + dz) % 2
    to = (((x + dx) % 4) * 4 + z2) * 2 + (core + dc) % 2
    return to, (dx + far + dz + dc) == 0


def turn_kernel(
    volt_hbm, taps_hbm, flags_hbm, steer_hbm, dirs_hbm, dft_hbm,
    spec_hbm, weight_hbm,
    volt, filt, stage, parcels, table, weights, dft, keep, taps_ref, flags_ref, dirs_ref,
    load_sem, send_sem, recv_sem, steer_send, steer_recv, local_sem,
):
    me, band = lax.axis_index("stn"), lax.axis_index("band")
    row, partner = band % 4, (band + 4) % BANDS
    column_peers = [(band // 4) * 4 + (row + d) % 4 for d in (1, 2, 3)]

    barrier = pltpu.get_barrier_semaphore()
    for b in [partner] + column_peers:
        pl.semaphore_signal(barrier, inc=1, device_id=(me, b), device_id_type=MESH)

    def greet(to, carry):
        @pl.when(to != me)
        def _():
            pl.semaphore_signal(barrier, inc=1, device_id=(to, band), device_id_type=MESH)

        return carry

    lax.fori_loop(0, STN, greet, 0)

    load_taps = pltpu.make_async_copy(taps_hbm, taps_ref, load_sem.at[5])
    load_flags = pltpu.make_async_copy(flags_hbm, flags_ref, load_sem.at[6])
    load_dirs = pltpu.make_async_copy(dirs_hbm, dirs_ref, load_sem.at[7])
    for copy in (load_taps, load_flags, load_dirs):
        copy.start()
    loads = []
    for s in range(2):
        for part, (start, size) in enumerate(((0, FIRST_COLS), (FIRST_COLS, SAMPLES - FIRST_COLS))):
            loads.append(pltpu.make_async_copy(
                volt_hbm.at[0, s, :, pl.ds(start, size)],
                volt.at[s, :, pl.ds(start, size)],
                load_sem.at[2 * s + part]))
    for copy in loads:
        copy.start()
    load_dft = pltpu.make_async_copy(dft_hbm, dft, load_sem.at[4])
    load_dft.start()

    def block(b):
        return table.at[pl.ds(pl.multiple_of(b * 512, 512), 512)]

    own_block = pltpu.make_async_copy(steer_hbm, block(band), local_sem.at[0])
    own_block.start()

    def filter_frames(s, first):
        def step(n, carry):
            f0 = first + n * BLOCK_FRAMES
            for h in range(2):
                coef = [taps_ref[t : t + 1, h * 128 : (h + 1) * 128] for t in range(TAPS)]
                acc = [None] * BLOCK_FRAMES
                for g in range(BLOCK_FRAMES + TAPS - 1):
                    at = pl.multiple_of((f0 + g) * CHAN + h * 128, 128)
                    x = volt[s, :, pl.ds(at, 128)].astype(F32)
                    for f in range(max(0, g - TAPS + 1), min(BLOCK_FRAMES - 1, g) + 1):
                        term = coef[g - f] * x
                        acc[f] = term if acc[f] is None else acc[f] + term
                for f in range(BLOCK_FRAMES):
                    to = pl.multiple_of((f0 + f) * INPUTS_HERE, INPUTS_HERE)
                    filt[s, h, pl.ds(to, INPUTS_HERE), :] = acc[f]
            return carry

        lax.fori_loop(0, HALF_FRAMES // BLOCK_FRAMES, step, 0)

    pl.semaphore_wait(barrier, STN - 1 + 4)
    steer_sends = []
    for n, b in enumerate([partner] + column_peers):
        steer_sends.append(pltpu.make_async_remote_copy(
            src_ref=steer_hbm, dst_ref=block(band),
            send_sem=steer_send.at[n], recv_sem=steer_recv.at[n],
            device_id=(me, b), device_id_type=MESH))
    for copy in steer_sends:
        copy.start()

    load_taps.wait()
    loads[0].wait()
    filter_frames(0, 0)
    loads[1].wait()
    filter_frames(0, HALF_FRAMES)
    loads[2].wait()
    filter_frames(1, 0)
    loads[3].wait()
    filter_frames(1, HALF_FRAMES)

    load_flags.wait()
    lines = lax.broadcasted_iota(jnp.int32, (INPUTS_HERE, 128), 0)
    mask = jnp.zeros((INPUTS_HERE, 128), jnp.int32)
    for i in range(INPUTS_HERE):
        mask = jnp.where(lines == i, flags_ref[i], mask)
    keep[...] = mask.astype(F32)

    load_dft.wait()

    rows = []
    for i in range(INPUTS_HERE):
        parts = [filt[s, h, pl.ds(i, FRAMES, stride=INPUTS_HERE), :] for s in range(2) for h in range(2)]
        rows.append(jnp.concatenate(parts, axis=1).astype(BF16))
    out = lax.dot_general(dft[...], jnp.concatenate(rows, axis=0), (((1,), (1,)), ((), ())),
                          preferred_element_type=F32)
    for i in range(INPUTS_HERE):
        stage[pl.ds(i, 2 * CHAN, stride=INPUTS_HERE), :] = out[:, i * 128 : (i + 1) * 128]

    here_rows = pl.ds(pl.multiple_of(me * INPUTS_HERE, INPUTS_HERE), INPUTS_HERE)

    def parcel(m, to):
        return pltpu.make_async_remote_copy(
            src_ref=parcels.at[m], dst_ref=spec_hbm.at[:, here_rows, :],
            send_sem=send_sem.at[m], recv_sem=recv_sem.at[m],
            device_id=(to, band), device_id_type=MESH)

    def own_parcel(m):
        return pltpu.make_async_copy(parcels.at[m], spec_hbm.at[:, here_rows, :], local_sem.at[1])

    def send(m, carry):
        to, here = peer(m)
        kept = keep[...]
        for j in range(CHAN_HERE):
            for o in range(2):
                at = pl.multiple_of(to * 256 + (o * CHAN_HERE + j) * INPUTS_HERE, INPUTS_HERE)
                tile = stage[pl.ds(at, INPUTS_HERE), :] * kept
                parcels[m, j, :, o * 128 : (o + 1) * 128] = tile.astype(BF16)

        @pl.when(here)
        def _():
            own_parcel(m).start()

        @pl.when(jnp.logical_not(here))
        def _():
            parcel(m, to).start()

        return carry

    lax.fori_loop(0, STN, send, 0)

    steer_sends[0].wait_recv()
    forwards = []
    for n, b in enumerate(column_peers):
        forwards.append(pltpu.make_async_remote_copy(
            src_ref=block(partner), dst_ref=block(partner),
            send_sem=steer_send.at[4 + n], recv_sem=steer_recv.at[4 + n],
            device_id=(me, b), device_id_type=MESH))
    for copy in forwards:
        copy.start()
    own_block.wait()
    for copy in steer_sends[1:] + forwards:
        copy.wait_recv()

    def widen(n, carry):
        at = pl.multiple_of(n * 256, 256)
        rows = table[pl.ds(at, 256), :].astype(F32)
        stage[pl.ds(at, 256), :] = rows[:, :128]
        stage[pl.ds(pl.multiple_of(4096 + n * 256, 256), 256), :] = rows[:, 128:]
        return carry

    lax.fori_loop(0, 16, widen, 0)
    load_dirs.wait()
    chosen = lax.broadcasted_iota(jnp.int32, (DIRS, BEAMS), 0) == dirs_ref[...]
    chosen = jnp.transpose(chosen.astype(F32)).astype(BF16)
    pairs = (lax.broadcasted_iota(jnp.int32, (STATIONS, INPUTS), 1) // 2
             == lax.broadcasted_iota(jnp.int32, (STATIONS, INPUTS), 0)).astype(F32).astype(BF16)

    def pick(n, carry):
        for o in range(2):
            halves = [stage[pl.ds(h * 4096 + o * CHAN_HERE + n, DIRS, stride=16), :] for h in range(2)]
            rows = jnp.concatenate(halves, axis=1).astype(BF16)
            picked = jnp.dot(chosen, rows, preferred_element_type=F32).astype(BF16)
            spread = jnp.dot(picked, pairs, preferred_element_type=F32)
            weights[n, o * BEAMS : (o + 1) * BEAMS, :] = spread.astype(BF16)
        return carry

    lax.fori_loop(0, CHAN_HERE, pick, 0)
    out_weights = pltpu.make_async_copy(weights, weight_hbm, local_sem.at[2])
    out_weights.start()

    for copy in steer_sends + forwards:
        copy.wait_send()

    def finish(m, carry):
        to, here = peer(m)

        @pl.when(here)
        def _():
            own_parcel(m).wait()

        @pl.when(jnp.logical_not(here))
        def _():
            parcel(m, to).wait()

        return carry

    lax.fori_loop(0, STN, finish, 0)
    out_weights.wait()


def form_kernel(spec_ref, weight_ref, vis_hbm, beam_hbm, vis, beam, vis_sem, beam_sem):
    nt = (((1,), (1,)), ((), ()))
    scale = 1.0 / FRAMES
    lane = lax.broadcasted_iota(jnp.int32, (2 * BEAMS, INPUTS), 1)
    writes = []
    for c in range(CHAN_HERE):
        rows = spec_ref[c]
        real, imag = rows[:, :FRAMES], rows[:, FRAMES:]
        for o in range(2):
            left = rows if o == 0 else jnp.concatenate([imag, -real], axis=1)
            products = lax.dot_general(left, rows, nt, preferred_element_type=F32)
            vis[c, o] = (products * scale).astype(BF16)
            writes.append(pltpu.make_async_copy(vis.at[c, o], vis_hbm.at[0, c, o], vis_sem.at[c, o]))
            writes[-1].start()
        weight = weight_ref[c]
        for p in range(2):
            mine = jnp.where(lane % 2 == p, weight, jnp.zeros_like(weight))
            formed = jnp.dot(mine, rows, preferred_element_type=F32)
            rr, ri = formed[:BEAMS, :FRAMES], formed[:BEAMS, FRAMES:]
            ir, ii = formed[BEAMS:, :FRAMES], formed[BEAMS:, FRAMES:]
            beam[c, 0, p] = (rr - ii).astype(BF16)
            beam[c, 1, p] = (ri + ir).astype(BF16)
        writes.append(pltpu.make_async_copy(beam.at[c], beam_hbm.at[0, c], beam_sem.at[c]))
        writes[-1].start()
    for copy in writes:
        copy.wait()


def body(dft, voltages, taps, flags, steer, beam_dirs):
    hbm = pl.BlockSpec(memory_space=pltpu.HBM)
    anywhere = pl.BlockSpec(memory_space=pl.ANY)
    vmem = pl.BlockSpec(memory_space=pltpu.VMEM)
    spectra, weights = pl.pallas_call(
        turn_kernel,
        out_shape=(
            jax.ShapeDtypeStruct((CHAN_HERE, INPUTS, 2 * FRAMES), BF16),
            jax.ShapeDtypeStruct((CHAN_HERE, 2 * BEAMS, INPUTS), BF16),
        ),
        in_specs=[hbm] * 6,
        out_specs=(anywhere, anywhere),
        scratch_shapes=[
            pltpu.VMEM((2, INPUTS_HERE, SAMPLES), BF16),
            pltpu.VMEM((2, 2, FRAMES * INPUTS_HERE, 128), F32),
            pltpu.VMEM((2 * CHAN * INPUTS_HERE, 128), F32),
            pltpu.VMEM((STN, CHAN_HERE, INPUTS_HERE, 2 * FRAMES), BF16),
            pltpu.VMEM((DIRS * 16, STATIONS), BF16),
            pltpu.VMEM((CHAN_HERE, 2 * BEAMS, INPUTS), BF16),
            pltpu.VMEM((2 * CHAN, 2 * CHAN), BF16),
            pltpu.VMEM((INPUTS_HERE, 128), F32),
            pltpu.VMEM((TAPS, CHAN), F32),
            pltpu.SMEM((INPUTS_HERE,), jnp.int32),
            pltpu.VMEM((1, BEAMS), jnp.int32),
            pltpu.SemaphoreType.DMA((8,)),
            pltpu.SemaphoreType.DMA((STN,)),
            pltpu.SemaphoreType.DMA((STN,)),
            pltpu.SemaphoreType.DMA((7,)),
            pltpu.SemaphoreType.DMA((7,)),
            pltpu.SemaphoreType.DMA((3,)),
        ],
        compiler_params=pltpu.CompilerParams(
            collective_id=0, has_side_effects=True, vmem_limit_bytes=36 * 2**20
        ),
        cost_estimate=pl.CostEstimate(
            flops=1_200_000_000, bytes_accessed=12_000_000, transcendentals=0
        ),
        name="turn",
    )(*[pltpu.with_memory_space_constraint(v, pltpu.HBM) for v in (
        voltages, taps, flags, steer.reshape(512, STATIONS), beam_dirs.reshape(1, BEAMS), dft)])
    return pl.pallas_call(
        form_kernel,
        out_shape=(
            jax.ShapeDtypeStruct((1, CHAN_HERE, 2, INPUTS, INPUTS), BF16),
            jax.ShapeDtypeStruct((1, CHAN_HERE, 2, 2, BEAMS, FRAMES), BF16),
        ),
        in_specs=[vmem, vmem],
        out_specs=(anywhere, anywhere),
        scratch_shapes=[
            pltpu.VMEM((CHAN_HERE, 2, INPUTS, INPUTS), BF16),
            pltpu.VMEM((CHAN_HERE, 2, 2, BEAMS, FRAMES), BF16),
            pltpu.SemaphoreType.DMA((CHAN_HERE, 2)),
            pltpu.SemaphoreType.DMA((CHAN_HERE,)),
        ],
        compiler_params=pltpu.CompilerParams(vmem_limit_bytes=32 * 2**20),
        cost_estimate=pl.CostEstimate(
            flops=3_300_000_000, bytes_accessed=14_000_000, transcendentals=0
        ),
        name="form",
    )(spectra, weights)


def solution(mesh):
    dft = dft_rows()

    def whole(*args):
        return jax.shard_map(
            functools.partial(body, jnp.asarray(dft)),
            mesh=mesh,
            in_specs=(P("band", None, "stn", None), P(), P("stn"), P("band", None, "stn", None), P()),
            out_specs=(P("band", "stn", None, None, None), P("band", "stn", None, None, None, None)),
            check_vma=False,
        )(*args)

    return whole
```

```python
import functools
import math

import jax
import jax.numpy as jnp
import numpy as np
from jax import lax
from jax.experimental import pallas as pl
from jax.experimental.pallas import tpu as pltpu
from jax.sharding import PartitionSpec as P

MESH = pl.DeviceIdType.MESH
BF16 = jnp.bfloat16
F32 = jnp.float32

STN = 32
BANDS = 8
INPUTS_HERE = 16
CHAN_HERE = 8
CHAN = 256
TAPS = 16
FRAMES = 128
SAMPLES = 36608
DIRS = 256
BEAMS = 128
STATIONS = 256
INPUTS = 512
HALF_FRAMES = 64
FIRST_COLS = (HALF_FRAMES + TAPS - 1) * CHAN
BLOCK_FRAMES = 16


def dft_rows():
    k = np.arange(CHAN)
    phase = (k[:, None] * k[None, :]) % CHAN
    angle = phase.astype(np.float32) * np.float32(2.0 * math.pi / CHAN)
    scale = np.float32(1.0 / math.sqrt(CHAN))
    c, s = np.cos(angle) * scale, np.sin(angle) * scale
    full = np.stack([np.stack([c, s], 0), np.stack([-s, c], 0)], 0)
    full = full.reshape(2, 2, CHAN, STN, CHAN_HERE).transpose(3, 0, 4, 1, 2)
    return full.reshape(2 * CHAN, 2 * CHAN).astype(jnp.bfloat16)


def peer(m):
    stn = lax.axis_index("stn")
    core, z, x = stn % 2, (stn // 2) % 4, stn // 8
    far, r = (m + 1) % 2, m // 2
    dc, dz, dx = r % 2, (r // 2) % 2, 3 - r // 4
    z2 = ((z // 2 + far) % 2) * 2 + (z % 2 + dz) % 2
    to = (((x + dx) % 4) * 4 + z2) * 2 + (core + dc) % 2
    return to, (dx + far + dz + dc) == 0


def turn_kernel(
    volt_hbm, taps_hbm, flags_hbm, steer_hbm, dirs_hbm, dft_hbm,
    spec_hbm, weight_hbm,
    volt, filt, stage, parcels, table, weights, dft, keep, taps_ref, flags_ref, dirs_ref,
    load_sem, send_sem, recv_sem, steer_send, steer_recv, local_sem,
):
    me, band = lax.axis_index("stn"), lax.axis_index("band")
    row, partner = band % 4, (band + 4) % BANDS
    column_peers = [(band // 4) * 4 + (row + d) % 4 for d in (1, 2, 3)]

    barrier = pltpu.get_barrier_semaphore()
    for b in [partner] + column_peers:
        pl.semaphore_signal(barrier, inc=1, device_id=(me, b), device_id_type=MESH)

    for n in range(1, STN):
        pl.semaphore_signal(barrier, inc=1, device_id=((me + n) % STN, band), device_id_type=MESH)

    load_taps = pltpu.make_async_copy(taps_hbm, taps_ref, load_sem.at[5])
    load_flags = pltpu.make_async_copy(flags_hbm, flags_ref, load_sem.at[6])
    load_dirs = pltpu.make_async_copy(dirs_hbm, dirs_ref, load_sem.at[7])
    for copy in (load_taps, load_flags, load_dirs):
        copy.start()
    loads = []
    for s in range(2):
        for part, (start, size) in enumerate(((0, FIRST_COLS), (FIRST_COLS, SAMPLES - FIRST_COLS))):
            loads.append(pltpu.make_async_copy(
                volt_hbm.at[0, s, :, pl.ds(start, size)],
                volt.at[s, :, pl.ds(start, size)],
                load_sem.at[2 * s + part]))
    for copy in loads:
        copy.start()
    load_dft = pltpu.make_async_copy(dft_hbm, dft, load_sem.at[4])
    load_dft.start()

    def block(b):
        return table.at[pl.ds(pl.multiple_of(b * 512, 512), 512)]

    own_block = pltpu.make_async_copy(steer_hbm, block(band), local_sem.at[0])
    own_block.start()

    def filter_frames(s, first):
        def step(n, carry):
            f0 = first + n * BLOCK_FRAMES
            for h in range(2):
                coef = [taps_ref[t : t + 1, h * 128 : (h + 1) * 128] for t in range(TAPS)]
                acc = [None] * BLOCK_FRAMES
                for g in range(BLOCK_FRAMES + TAPS - 1):
                    at = pl.multiple_of((f0 + g) * CHAN + h * 128, 128)
                    x = volt[s, :, pl.ds(at, 128)].astype(F32)
                    for f in range(max(0, g - TAPS + 1), min(BLOCK_FRAMES - 1, g) + 1):
                        term = coef[g - f] * x
                        acc[f] = term if acc[f] is None else acc[f] + term
                for f in range(BLOCK_FRAMES):
                    to = pl.multiple_of((f0 + f) * INPUTS_HERE, INPUTS_HERE)
                    filt[s, h, pl.ds(to, INPUTS_HERE), :] = acc[f]
            return carry

        lax.fori_loop(0, HALF_FRAMES // BLOCK_FRAMES, step, 0)

    pl.semaphore_wait(barrier, STN - 1 + 4)
    steer_sends = []
    for n, b in enumerate([partner] + column_peers):
        steer_sends.append(pltpu.make_async_remote_copy(
            src_ref=steer_hbm, dst_ref=block(band),
            send_sem=steer_send.at[n], recv_sem=steer_recv.at[n],
            device_id=(me, b), device_id_type=MESH))
    for copy in steer_sends:
        copy.start()

    load_taps.wait()
    loads[0].wait()
    filter_frames(0, 0)
    loads[1].wait()
    filter_frames(0, HALF_FRAMES)
    loads[2].wait()
    filter_frames(1, 0)
    loads[3].wait()
    filter_frames(1, HALF_FRAMES)

    load_flags.wait()
    lines = lax.broadcasted_iota(jnp.int32, (INPUTS_HERE, 128), 0)
    mask = jnp.zeros((INPUTS_HERE, 128), jnp.int32)
    for i in range(INPUTS_HERE):
        mask = jnp.where(lines == i, flags_ref[i], mask)
    keep[...] = mask.astype(F32)

    load_dft.wait()

    rows = []
    for i in range(INPUTS_HERE):
        parts = [filt[s, h, pl.ds(i, FRAMES, stride=INPUTS_HERE), :] for s in range(2) for h in range(2)]
        rows.append(jnp.concatenate(parts, axis=1).astype(BF16))
    out = lax.dot_general(dft[...], jnp.concatenate(rows, axis=0), (((1,), (1,)), ((), ())),
                          preferred_element_type=F32)
    for i in range(INPUTS_HERE):
        stage[pl.ds(i, 2 * CHAN, stride=INPUTS_HERE), :] = out[:, i * 128 : (i + 1) * 128]

    here_rows = pl.ds(pl.multiple_of(me * INPUTS_HERE, INPUTS_HERE), INPUTS_HERE)

    def parcel(m, to):
        return pltpu.make_async_remote_copy(
            src_ref=parcels.at[m], dst_ref=spec_hbm.at[:, here_rows, :],
            send_sem=send_sem.at[m], recv_sem=recv_sem.at[m],
            device_id=(to, band), device_id_type=MESH)

    def own_parcel(m):
        return pltpu.make_async_copy(parcels.at[m], spec_hbm.at[:, here_rows, :], local_sem.at[1])

    def send(m, carry):
        to, here = peer(m)
        kept = keep[...]
        for j in range(CHAN_HERE):
            for o in range(2):
                at = pl.multiple_of(to * 256 + (o * CHAN_HERE + j) * INPUTS_HERE, INPUTS_HERE)
                tile = stage[pl.ds(at, INPUTS_HERE), :] * kept
                parcels[m, j, :, o * 128 : (o + 1) * 128] = tile.astype(BF16)

        @pl.when(here)
        def _():
            own_parcel(m).start()

        @pl.when(jnp.logical_not(here))
        def _():
            parcel(m, to).start()

        return carry

    lax.fori_loop(0, STN, send, 0)

    steer_sends[0].wait_recv()
    forwards = []
    for n, b in enumerate(column_peers):
        forwards.append(pltpu.make_async_remote_copy(
            src_ref=block(partner), dst_ref=block(partner),
            send_sem=steer_send.at[4 + n], recv_sem=steer_recv.at[4 + n],
            device_id=(me, b), device_id_type=MESH))
    for copy in forwards:
        copy.start()
    own_block.wait()
    for copy in steer_sends[1:] + forwards:
        copy.wait_recv()

    def widen(n, carry):
        at = pl.multiple_of(n * 256, 256)
        rows = table[pl.ds(at, 256), :].astype(F32)
        stage[pl.ds(at, 256), :] = rows[:, :128]
        stage[pl.ds(pl.multiple_of(4096 + n * 256, 256), 256), :] = rows[:, 128:]
        return carry

    lax.fori_loop(0, 16, widen, 0)
    load_dirs.wait()
    chosen = lax.broadcasted_iota(jnp.int32, (DIRS, BEAMS), 0) == dirs_ref[...]
    chosen = jnp.transpose(chosen.astype(F32)).astype(BF16)
    pairs = (lax.broadcasted_iota(jnp.int32, (STATIONS, INPUTS), 1) // 2
             == lax.broadcasted_iota(jnp.int32, (STATIONS, INPUTS), 0)).astype(F32).astype(BF16)

    def pick(n, carry):
        for o in range(2):
            halves = [stage[pl.ds(h * 4096 + o * CHAN_HERE + n, DIRS, stride=16), :] for h in range(2)]
            rows = jnp.concatenate(halves, axis=1).astype(BF16)
            picked = jnp.dot(chosen, rows, preferred_element_type=F32).astype(BF16)
            spread = jnp.dot(picked, pairs, preferred_element_type=F32)
            weights[n, o * BEAMS : (o + 1) * BEAMS, :] = spread.astype(BF16)
        return carry

    lax.fori_loop(0, CHAN_HERE, pick, 0)
    out_weights = pltpu.make_async_copy(weights, weight_hbm, local_sem.at[2])
    out_weights.start()

    for copy in steer_sends + forwards:
        copy.wait_send()

    def finish(m, carry):
        to, here = peer(m)

        @pl.when(here)
        def _():
            own_parcel(m).wait()

        @pl.when(jnp.logical_not(here))
        def _():
            parcel(m, to).wait()

        return carry

    lax.fori_loop(0, STN, finish, 0)
    out_weights.wait()


def form_kernel(spec_ref, weight_ref, vis_hbm, beam_hbm, vis, beam, vis_sem, beam_sem):
    nt = (((1,), (1,)), ((), ()))
    scale = 1.0 / FRAMES
    lane = lax.broadcasted_iota(jnp.int32, (2 * BEAMS, INPUTS), 1)
    writes = []
    for c in range(CHAN_HERE):
        rows = spec_ref[c]
        real, imag = rows[:, :FRAMES], rows[:, FRAMES:]
        for o in range(2):
            left = rows if o == 0 else jnp.concatenate([imag, -real], axis=1)
            products = lax.dot_general(left, rows, nt, preferred_element_type=F32)
            vis[c, o] = (products * scale).astype(BF16)
            writes.append(pltpu.make_async_copy(vis.at[c, o], vis_hbm.at[0, c, o], vis_sem.at[c, o]))
            writes[-1].start()
        weight = weight_ref[c]
        for p in range(2):
            mine = jnp.where(lane % 2 == p, weight, jnp.zeros_like(weight))
            formed = jnp.dot(mine, rows, preferred_element_type=F32)
            rr, ri = formed[:BEAMS, :FRAMES], formed[:BEAMS, FRAMES:]
            ir, ii = formed[BEAMS:, :FRAMES], formed[BEAMS:, FRAMES:]
            beam[c, 0, p] = (rr - ii).astype(BF16)
            beam[c, 1, p] = (ri + ir).astype(BF16)
        writes.append(pltpu.make_async_copy(beam.at[c], beam_hbm.at[0, c], beam_sem.at[c]))
        writes[-1].start()
    for copy in writes:
        copy.wait()


def body(dft, voltages, taps, flags, steer, beam_dirs):
    hbm = pl.BlockSpec(memory_space=pltpu.HBM)
    anywhere = pl.BlockSpec(memory_space=pl.ANY)
    vmem = pl.BlockSpec(memory_space=pltpu.VMEM)
    spectra, weights = pl.pallas_call(
        turn_kernel,
        out_shape=(
            jax.ShapeDtypeStruct((CHAN_HERE, INPUTS, 2 * FRAMES), BF16),
            jax.ShapeDtypeStruct((CHAN_HERE, 2 * BEAMS, INPUTS), BF16),
        ),
        in_specs=[hbm] * 6,
        out_specs=(anywhere, anywhere),
        scratch_shapes=[
            pltpu.VMEM((2, INPUTS_HERE, SAMPLES), BF16),
            pltpu.VMEM((2, 2, FRAMES * INPUTS_HERE, 128), F32),
            pltpu.VMEM((2 * CHAN * INPUTS_HERE, 128), F32),
            pltpu.VMEM((STN, CHAN_HERE, INPUTS_HERE, 2 * FRAMES), BF16),
            pltpu.VMEM((DIRS * 16, STATIONS), BF16),
            pltpu.VMEM((CHAN_HERE, 2 * BEAMS, INPUTS), BF16),
            pltpu.VMEM((2 * CHAN, 2 * CHAN), BF16),
            pltpu.VMEM((INPUTS_HERE, 128), F32),
            pltpu.VMEM((TAPS, CHAN), F32),
            pltpu.SMEM((INPUTS_HERE,), jnp.int32),
            pltpu.VMEM((1, BEAMS), jnp.int32),
            pltpu.SemaphoreType.DMA((8,)),
            pltpu.SemaphoreType.DMA((STN,)),
            pltpu.SemaphoreType.DMA((STN,)),
            pltpu.SemaphoreType.DMA((7,)),
            pltpu.SemaphoreType.DMA((7,)),
            pltpu.SemaphoreType.DMA((3,)),
        ],
        compiler_params=pltpu.CompilerParams(
            collective_id=0, has_side_effects=True, vmem_limit_bytes=36 * 2**20
        ),
        cost_estimate=pl.CostEstimate(
            flops=1_200_000_000, bytes_accessed=12_000_000, transcendentals=0
        ),
        name="turn",
    )(*[pltpu.with_memory_space_constraint(v, pltpu.HBM) for v in (
        voltages, taps, flags, steer.reshape(512, STATIONS), beam_dirs.reshape(1, BEAMS), dft)])
    return pl.pallas_call(
        form_kernel,
        out_shape=(
            jax.ShapeDtypeStruct((1, CHAN_HERE, 2, INPUTS, INPUTS), BF16),
            jax.ShapeDtypeStruct((1, CHAN_HERE, 2, 2, BEAMS, FRAMES), BF16),
        ),
        in_specs=[vmem, vmem],
        out_specs=(anywhere, anywhere),
        scratch_shapes=[
            pltpu.VMEM((CHAN_HERE, 2, INPUTS, INPUTS), BF16),
            pltpu.VMEM((CHAN_HERE, 2, 2, BEAMS, FRAMES), BF16),
            pltpu.SemaphoreType.DMA((CHAN_HERE, 2)),
            pltpu.SemaphoreType.DMA((CHAN_HERE,)),
        ],
        compiler_params=pltpu.CompilerParams(vmem_limit_bytes=32 * 2**20),
        cost_estimate=pl.CostEstimate(
            flops=3_300_000_000, bytes_accessed=14_000_000, transcendentals=0
        ),
        name="form",
    )(spectra, weights)


def solution(mesh):
    dft = dft_rows()

    def whole(*args):
        return jax.shard_map(
            functools.partial(body, jnp.asarray(dft)),
            mesh=mesh,
            in_specs=(P("band", None, "stn", None), P(), P("stn"), P("band", None, "stn", None), P()),
            out_specs=(P("band", "stn", None, None, None), P("band", "stn", None, None, None, None)),
            check_vma=False,
        )(*args)

    return whole
```
